32 devices in a mesh: expert: 4 (over y, x), dp: 4 (over z), shadow: 2 (over core).
Axes of the slice: x: 2, y: 2, z: 4, core: 2. Of those that a mesh axis runs over, the one named last changes fastest.
Arguments:
- tokens: bfloat16 [2048, 3584], P(('expert', 'dp')), may hold values from -6 to 6
- expert_ids: int32 [2048, 8], P(('expert', 'dp')), may hold values from 0 to 255, as said below
- gate_values: float32 [2048, 8], P(('expert', 'dp')), may hold values from 0.1 to 1
- cotangent: bfloat16 [2048, 3584], P(('expert', 'dp')), may hold values from -6 to 6
- w_gate: bfloat16 [4, 3584, 1024], P('expert', None, ('dp', 'shadow')), may hold values from -0.09375 to 0.09375
- w_up: bfloat16 [4, 3584, 1024], P('expert', None, ('dp', 'shadow')), may hold values from -0.09375 to 0.09375
- w_down: bfloat16 [4, 1024, 3584], P('expert', ('dp', 'shadow')), may hold values from -0.1875 to 0.1875
Outputs:
- token_grad: bfloat16 [2048, 3584], P(('expert', 'dp'))
- grad_gate: bfloat16 [4, 3584, 1024], P('expert', None, ('dp', 'shadow'))
- grad_up: bfloat16 [4, 3584, 1024], P('expert', None, ('dp', 'shadow'))
- grad_down: bfloat16 [4, 1024, 3584], P('expert', ('dp', 'shadow'))
The draws below stay inside these ranges and needn't reach their ends.
Inputs may be any that keep to these rules, and one draw needn't show every extreme that they name: `expert_ids`: each row names 8 different experts, exactly one of them below 4. In each aligned block of 128 rows (the rows of one device) no expert below 4 is named by more than 64 rows, and one of them, the same in every block, is named by exactly 64 rows.
All inputs are finite; a program needn't handle non-finite values.
Results may differ from the reference program's by a relative error of at most 0.0065.
Values may be sent and summed in bfloat16 or wider, within the bound.
No kernel may reach another device: no remote copies, remote signals or barrier semaphores. Data moves between devices by JAX's collectives and lax.ppermute only.
A program may use at most 128 MiB of HBM per device.

```python
import math
import jax
import jax.numpy as jnp
from jax import lax

D = 3584
FF = 1024
TOPK = 8
ALL_EXPERTS = 256
TOK_DEV = 128
EXPERTS = 4
CAP = 64
TOKENS = 2048
N_DP = 4
N_SHADOW = 2


def draw_expert_ids(key, part):
    hot_key, block_key, row_key = jax.random.split(key, 3)
    block_count = TOKENS // TOK_DEV
    hot_expert = jax.random.randint(hot_key, (), 0, EXPERTS).astype(jnp.int32)
    cold_slots = (EXPERTS - 1) * CAP

    def one_block(some_key):
        pick_key, order_key = jax.random.split(some_key)
        shuffled = jax.random.permutation(pick_key, cold_slots)[:TOK_DEV - CAP]
        cold_expert = (shuffled // CAP).astype(jnp.int32)
        cold_expert = cold_expert + (cold_expert >= hot_expert).astype(jnp.int32)
        chosen = jnp.concatenate([jnp.full((CAP,), hot_expert, jnp.int32), cold_expert])
        order = jax.random.permutation(order_key, TOK_DEV)
        return chosen[order]
    window_expert = jax.vmap(one_block)(jax.random.split(block_key, block_count)).reshape(TOKENS)
    group_count = ALL_EXPERTS // EXPERTS

    def row_ids(some_key, expert_here):
        extra_key, column_key = jax.random.split(some_key)
        extra = (jax.random.permutation(extra_key, group_count - 1)[:TOPK - 1] + 1).astype(jnp.int32)
        multiples = jnp.concatenate([jnp.zeros((1,), jnp.int32), extra])
        multiples = jax.random.permutation(column_key, multiples)
        return (expert_here + EXPERTS * multiples).astype(jnp.int32)
    return jax.vmap(row_ids)(jax.random.split(row_key, TOKENS), window_expert)


def block_levels(key, extent, cuts, least, largest):
    gain, own = 1.0, jax.random.fold_in(key, 6)
    for axis_at, parts in cuts:
        draws = jnp.exp(jax.random.uniform(jax.random.fold_in(own, axis_at), (parts,), jnp.float32, least / len(cuts), largest / len(cuts)))
        gain = gain * jnp.repeat(draws, extent[axis_at] // parts).reshape([-1 if axis == axis_at else 1 for axis in range(len(extent))])
    return gain


def normal_values(key, dims, scale, limit, cuts=(), kind=jnp.bfloat16):
    array = scale * jax.random.normal(key, dims, jnp.float32)
    if cuts:
        array = array * block_levels(key, dims, cuts, -0.22, 0.18)
    return jnp.clip(array, -limit, limit).astype(kind)


def setup_inputs(seed: int = 0) -> dict:
    seeds = jax.random.split(jax.random.key(seed), 8)
    tokens = normal_values(seeds[0], (TOKENS, D), 1.0, 6.0, ((0, 16),))
    expert_ids = draw_expert_ids(jax.random.fold_in(seeds[7], 71), 0)
    gate_values = jnp.clip(jnp.exp(math.log(1.0) - 2.3025851 * jax.random.uniform(seeds[2], (TOKENS, TOPK), jnp.float32) ** block_levels(seeds[2], (TOKENS, TOPK), ((0, 16),), -0.2, 0.2)), 0.1, 1.0)
    cotangent = normal_values(seeds[3], (TOKENS, D), 1.0, 6.0, ((0, 16),))
    w_gate = normal_values(seeds[4], (EXPERTS, D, FF), D ** -0.5, 0.09375, ((0, 4), (2, 8)))
    w_up = normal_values(seeds[5], (EXPERTS, D, FF), D ** -0.5, 0.09375, ((0, 4), (2, 8)))
    w_down = normal_values(seeds[6], (EXPERTS, FF, D), FF ** -0.5, 0.1875, ((0, 4), (1, 8)))
    return {"tokens": tokens, "expert_ids": expert_ids, "gate_values": gate_values, "cotangent": cotangent, "w_gate": w_gate, "w_up": w_up, "w_down": w_down}


def expert_pass(operands):
    slot_tokens, slot_cotan, gate_weight, up_weight, down_weight = operands
    blocks = N_DP * N_SHADOW
    unit_count = FF // blocks
    slot_count = slot_tokens.shape[0]
    gate_pre = jnp.dot(slot_tokens, gate_weight, preferred_element_type=jnp.float32)
    up_pre = jnp.dot(slot_tokens, up_weight, preferred_element_type=jnp.float32)
    sigmoid_gate = jax.nn.sigmoid(gate_pre)
    silu_gate = gate_pre * sigmoid_gate
    hidden = (silu_gate * up_pre).astype(jnp.bfloat16)
    hidden_grad = jnp.dot(slot_cotan, down_weight.T, preferred_element_type=jnp.float32)
    gate_grad = (hidden_grad * up_pre * sigmoid_gate * (1.0 + gate_pre * (1.0 - sigmoid_gate))).astype(jnp.bfloat16)
    up_grad = (hidden_grad * silu_gate).astype(jnp.bfloat16)
    grad_gate = jnp.dot(slot_tokens.T, gate_grad, preferred_element_type=jnp.float32).astype(jnp.bfloat16)
    grad_up = jnp.dot(slot_tokens.T, up_grad, preferred_element_type=jnp.float32).astype(jnp.bfloat16)
    grad_down = jnp.dot(hidden.T, slot_cotan, preferred_element_type=jnp.float32).astype(jnp.bfloat16)
    gate_blocks = gate_grad.astype(jnp.float32).reshape(slot_count, blocks, unit_count)
    up_blocks = up_grad.astype(jnp.float32).reshape(slot_count, blocks, unit_count)
    gate_table = gate_weight.astype(jnp.float32).reshape(D, blocks, unit_count)
    up_table = up_weight.astype(jnp.float32).reshape(D, blocks, unit_count)
    block_terms = jnp.einsum("rju,dju->rjd", gate_blocks, gate_table) + jnp.einsum("rju,dju->rjd", up_blocks, up_table)
    rounded = lax.optimization_barrier(block_terms.astype(jnp.bfloat16))
    row_sums = jnp.sum(rounded.astype(jnp.float32), axis=1)
    return grad_gate, grad_up, grad_down, row_sums


def reference(tokens, expert_ids, gate_values, cotangent, w_gate, w_up, w_down):
    source_count = TOKENS // TOK_DEV
    in_window = expert_ids < EXPERTS
    window_expert = jnp.sum(jnp.where(in_window, expert_ids, 0), axis=1).astype(jnp.int32)
    route_gate = jnp.sum(jnp.where(in_window, gate_values, jnp.zeros_like(gate_values)), axis=1)
    member = (window_expert[:, None] == jnp.arange(EXPERTS, dtype=jnp.int32)[None, :]).astype(jnp.int32)
    member_blocks = member.reshape(source_count, TOK_DEV, EXPERTS)
    earlier = jnp.cumsum(member_blocks, axis=1) - member_blocks
    slot_rank = jnp.sum(earlier * member_blocks, axis=2).reshape(TOKENS).astype(jnp.int32)
    source_index = (jnp.arange(TOKENS, dtype=jnp.int32) // TOK_DEV).astype(jnp.int32)
    slot_index = (source_index * CAP + slot_rank).astype(jnp.int32)
    scaled_cotangent = (route_gate[:, None] * cotangent.astype(jnp.float32)).astype(jnp.bfloat16)
    slot_width = source_count * CAP
    slot_tokens = jnp.zeros((EXPERTS, slot_width, D), tokens.dtype).at[window_expert, slot_index].set(tokens)
    slot_cotan = jnp.zeros((EXPERTS, slot_width, D), scaled_cotangent.dtype).at[window_expert, slot_index].set(scaled_cotangent)
    grad_gate, grad_up, grad_down, row_sums = lax.map(expert_pass, (slot_tokens, slot_cotan, w_gate, w_up, w_down))
    token_grad = row_sums[window_expert, slot_index].astype(jnp.bfloat16)
    return token_grad, grad_gate, grad_up, grad_down
```

```python
import jax
import jax.numpy as jnp
from jax import lax
from jax.sharding import PartitionSpec as P

CONTRACT_LAST = (((1,), (1,)), ((), ()))
CONTRACT_FIRST = (((0,), (0,)), ((), ()))
MOST_PERMUTES = 8


def dot(a, b, dims=(((1,), (0,)), ((), ()))):
    return lax.dot_general(a, b, dims, preferred_element_type=jnp.float32)


def select(one_hot, rows):
    return dot(one_hot, rows).astype(jnp.bfloat16)


def flip(value, axis, mask):
    size = lax.axis_size(axis)
    return lax.ppermute(value, axis, [(i, i ^ mask) for i in range(size)])


def step_on(value, axis):
    size = lax.axis_size(axis)
    return lax.ppermute(value, axis, [(i, (i + 1) % size) for i in range(size)])


def by_permutes(axis):
    size = lax.axis_size(axis)
    return size & (size - 1) == 0 and size <= MOST_PERMUTES


def peers_of(axis):
    size = lax.axis_size(axis)
    order = jnp.arange(size, dtype=jnp.int32)
    if by_permutes(axis):
        return order ^ lax.axis_index(axis)
    return order


def exchange(parts, axis):
    if by_permutes(axis):
        return [parts[0]] + [flip(parts[m], axis, m) for m in range(1, len(parts))]
    got = lax.all_to_all(jnp.stack(parts), axis, split_axis=0, concat_axis=0, tiled=True)
    return [got[m] for m in range(len(parts))]


def on_device(tokens, expert_ids, gate_values, cotangent, w_gate, w_up, w_down):
    token_count, model_width = tokens.shape
    groups = lax.axis_size("expert")
    dp_count = lax.axis_size("dp")
    cores = lax.axis_size("shadow")
    experts = w_gate.shape[0] * groups
    capacity = max(2, 2 * token_count // experts)
    seats = -(-capacity // cores)
    row_count = token_count // cores
    unit_count = w_gate.shape[2]
    core = lax.axis_index("shadow")
    dp_index = lax.axis_index("dp")

    def chip_weights(weight, axis):
        return [weight] + [flip(weight, "shadow", m) for m in range(1, cores)]

    gate_parts = chip_weights(w_gate[0], 1)
    up_parts = chip_weights(w_up[0], 1)
    down_parts = chip_weights(w_down[0], 0)
    in_weight = jnp.concatenate(gate_parts + up_parts, axis=1)
    down_weight = jnp.concatenate(down_parts, axis=0)
    chip_units = cores * unit_count

    in_window = expert_ids < experts
    window_expert = jnp.sum(jnp.where(in_window, expert_ids, 0), axis=1)
    route_gate = jnp.sum(jnp.where(in_window, gate_values, 0.0), axis=1)
    key = window_expert * token_count + jnp.arange(token_count, dtype=jnp.int32)
    position = jnp.sum((key[None, :] < key[:, None]).astype(jnp.int32), axis=1)
    first = jnp.sum(
        (window_expert[None, :] < jnp.arange(experts + 1, dtype=jnp.int32)[:, None]).astype(jnp.int32),
        axis=1,
    )
    first_row = (first - core + cores - 1) // cores
    all_first = lax.all_gather(first_row, "dp", axis=0)
    scaled = (route_gate[:, None] * cotangent.astype(jnp.float32)).astype(jnp.bfloat16)
    row_ids = jnp.arange(row_count, dtype=jnp.int32)
    pick = (position[None, :] == (cores * row_ids + core)[:, None]).astype(jnp.bfloat16)
    rows = jnp.concatenate([select(pick, tokens), select(pick, scaled)], axis=1)

    peers = peers_of("expert")
    seat_ids = jnp.arange(seats, dtype=jnp.int32)

    def seating(block_first):
        start = block_first[peers]
        stop = block_first[peers + 1]
        wanted = start[:, None] + seat_ids[None, :]
        taken = (wanted[:, :, None] == row_ids) & (wanted < stop[:, None])[:, :, None]
        return taken.astype(jnp.bfloat16)

    seatings, slot_rows = [], []
    held = rows
    for k in range(dp_count):
        arriving = step_on(held, "dp") if k < dp_count - 1 else None
        if k == 0:
            block_first = first_row
        else:
            block_first = all_first[(dp_index - k) % dp_count]
        seat = seating(block_first)
        seatings.append(seat)
        got = exchange([select(seat[m], held) for m in range(groups)], "expert")
        slot_rows.append(jnp.concatenate(got, axis=0))
        held = arriving

    def work(slots):
        slot_tokens, slot_cotan = slots[:, :model_width], slots[:, model_width:]
        pre = dot(slot_tokens, in_weight)
        gate_pre, up_pre = pre[:, :chip_units], pre[:, chip_units:]
        sigmoid_gate = jax.nn.sigmoid(gate_pre)
        silu_gate = gate_pre * sigmoid_gate
        hidden = (silu_gate * up_pre).astype(jnp.bfloat16)
        hidden_grad = dot(slot_cotan, down_weight, CONTRACT_LAST)
        gate_grad = (
            hidden_grad * up_pre * sigmoid_gate * (1.0 + gate_pre * (1.0 - sigmoid_gate))
        ).astype(jnp.bfloat16)
        up_grad = (hidden_grad * silu_gate).astype(jnp.bfloat16)
        in_grad = jnp.concatenate([gate_grad, up_grad], axis=1)
        terms = dot(in_grad, in_weight, CONTRACT_LAST).astype(jnp.bfloat16)
        return hidden, in_grad, terms

    hiddens, in_grads, sums = [], [], []
    for k in range(dp_count):
        hidden, in_grad, terms = work(slot_rows[k])
        hiddens.append(hidden)
        in_grads.append(in_grad)
        got = exchange([terms[m * seats : (m + 1) * seats] for m in range(groups)], "expert")
        seat = seatings[k].reshape(groups * seats, row_count)
        sums.append(dot(seat, jnp.concatenate(got, axis=0), CONTRACT_FIRST))

    total = sums[1 % dp_count]
    for k in list(range(2, dp_count)) + ([0] if dp_count > 1 else []):
        total = sums[k] + step_on(total.astype(jnp.bfloat16), "dp").astype(jnp.float32)
    own = total.astype(jnp.bfloat16)
    halves = [own] + [flip(own, "shadow", m) for m in range(1, cores)]
    half_of = position % cores
    place = jnp.concatenate(
        [
            ((position // cores)[:, None] == row_ids[None, :]) & (half_of == core ^ m)[:, None]
            for m in range(cores)
        ],
        axis=1,
    ).astype(jnp.bfloat16)
    token_grad = select(place, jnp.concatenate(halves, axis=0))

    slots = jnp.concatenate(slot_rows, axis=0)
    hidden = jnp.concatenate(hiddens, axis=0)
    in_grad = jnp.concatenate(in_grads, axis=0)
    in_sums = dot(slots[:, :model_width], in_grad, CONTRACT_FIRST)
    down_sums = dot(hidden, slots[:, model_width:], CONTRACT_FIRST)

    def own_units(parts):
        total = parts[0]
        for m in range(1, cores):
            total = total + flip(parts[m].astype(jnp.bfloat16), "shadow", m).astype(jnp.float32)
        return total.astype(jnp.bfloat16)[None]

    def units(start):
        return slice(start * unit_count, (start + 1) * unit_count)

    grad_gate = own_units([in_sums[:, units(m)] for m in range(cores)])
    grad_up = own_units([in_sums[:, units(cores + m)] for m in range(cores)])
    grad_down = own_units([down_sums[units(m)] for m in range(cores)])
    return (token_grad, grad_gate, grad_up, grad_down)


def solution(mesh):
    placed = (
        P(("expert", "dp"), None),
        P(("expert", "dp"), None),
        P(("expert", "dp"), None),
        P(("expert", "dp"), None),
        P("expert", None, ("dp", "shadow")),
        P("expert", None, ("dp", "shadow")),
        P("expert", ("dp", "shadow"), None),
    )
    return jax.shard_map(
        on_device,
        mesh=mesh,
        in_specs=placed,
        out_specs=(
            P(("expert", "dp"), None),
            P("expert", None, ("dp", "shadow")),
            P("expert", None, ("dp", "shadow")),
            P("expert", ("dp", "shadow"), None),
        ),
        check_vma=False,
    )
```

```python
import jax
import jax.numpy as jnp
from jax import lax
from jax.sharding import PartitionSpec as P

CONTRACT_LAST = (((1,), (1,)), ((), ()))
CONTRACT_FIRST = (((0,), (0,)), ((), ()))
MOST_PERMUTES = 8
LANES = 128


def dot(a, b, dims=(((1,), (0,)), ((), ()))):
    return lax.dot_general(a, b, dims, preferred_element_type=jnp.float32)


def select(one_hot, rows):
    return dot(one_hot, rows).astype(jnp.bfloat16)


def flip(value, axis, mask):
    size = lax.axis_size(axis)
    return lax.ppermute(value, axis, [(i, i ^ mask) for i in range(size)])


def step_on(value, axis, step):
    size = lax.axis_size(axis)
    return lax.ppermute(value, axis, [(i, (i + step) % size) for i in range(size)])


def by_permutes(axis):
    size = lax.axis_size(axis)
    return size & (size - 1) == 0 and size <= MOST_PERMUTES


def peers_of(axis):
    size = lax.axis_size(axis)
    order = jnp.arange(size, dtype=jnp.int32)
    if by_permutes(axis):
        return order ^ lax.axis_index(axis)
    return order


def exchange(parts, axis):
    if by_permutes(axis):
        return [parts[0]] + [flip(parts[m], axis, m) for m in range(1, len(parts))]
    got = lax.all_to_all(jnp.stack(parts), axis, split_axis=0, concat_axis=0, tiled=True)
    return [got[m] for m in range(len(parts))]


def on_device(tokens, expert_ids, gate_values, cotangent, w_gate, w_up, w_down):
    token_count, model_width = tokens.shape
    groups = lax.axis_size("expert")
    dp_count = lax.axis_size("dp")
    cores = lax.axis_size("shadow")
    experts = w_gate.shape[0] * groups
    capacity = max(2, 2 * token_count // experts)
    seats = -(-capacity // cores)
    row_count = token_count // cores
    unit_count = w_gate.shape[2]
    core = lax.axis_index("shadow")

    def chip_weights(weight, axis):
        return [weight] + [flip(weight, "shadow", m) for m in range(1, cores)]

    gate_parts = chip_weights(w_gate[0], 1)
    up_parts = chip_weights(w_up[0], 1)
    down_parts = chip_weights(w_down[0], 0)
    in_weight = jnp.concatenate(gate_parts + up_parts, axis=1)
    down_weight = jnp.concatenate(down_parts, axis=0)
    chip_units = cores * unit_count

    in_window = expert_ids < experts
    window_expert = jnp.sum(jnp.where(in_window, expert_ids, 0), axis=1)
    route_gate = jnp.sum(jnp.where(in_window, gate_values, 0.0), axis=1)
    key = window_expert * token_count + jnp.arange(token_count, dtype=jnp.int32)
    position = jnp.sum((key[None, :] < key[:, None]).astype(jnp.int32), axis=1)
    first = jnp.sum(
        (window_expert[None, :] < jnp.arange(experts + 1, dtype=jnp.int32)[:, None]).astype(jnp.int32),
        axis=1,
    )
    first_row = (first - core + cores - 1) // cores
    scaled = (route_gate[:, None] * cotangent.astype(jnp.float32)).astype(jnp.bfloat16)
    row_ids = jnp.arange(row_count, dtype=jnp.int32)
    pick = (position[None, :] == (cores * row_ids + core)[:, None]).astype(jnp.bfloat16)
    here = (first_row[:-1, None] <= row_ids) & (row_ids < first_row[1:, None])
    row_expert = jnp.sum(jnp.where(here, jnp.arange(experts, dtype=jnp.int32)[:, None], 0), axis=0)
    row_rank = row_ids - jnp.sum(jnp.where(here, first_row[:-1, None], 0), axis=0)
    notes = jnp.stack([row_expert, row_rank]).astype(jnp.bfloat16)
    notes = jnp.pad(notes, ((0, row_count - 2), (0, -row_count % LANES)))
    rows = jnp.concatenate([select(pick, tokens), select(pick, scaled), notes], axis=1)

    peers = peers_of("expert")
    seat_ids = jnp.arange(seats, dtype=jnp.int32)

    def seating(block):
        notes = block[:2, 2 * model_width : 2 * model_width + row_count].astype(jnp.int32)
        taken = (notes[0] == peers[:, None, None]) & (notes[1] == seat_ids[None, :, None])
        return taken.astype(jnp.bfloat16)

    def spread(block):
        seat = seating(block)
        wide = block[:, : 2 * model_width]
        return seat, [select(seat[m], wide) for m in range(groups)]

    def work(slots):
        slot_tokens, slot_cotan = slots[:, :model_width], slots[:, model_width:]
        pre = dot(slot_tokens, in_weight)
        gate_pre, up_pre = pre[:, :chip_units], pre[:, chip_units:]
        sigmoid_gate = jax.nn.sigmoid(gate_pre)
        silu_gate = gate_pre * sigmoid_gate
        hidden = (silu_gate * up_pre).astype(jnp.bfloat16)
        hidden_grad = dot(slot_cotan, down_weight, CONTRACT_LAST)
        gate_grad = (
            hidden_grad * up_pre * sigmoid_gate * (1.0 + gate_pre * (1.0 - sigmoid_gate))
        ).astype(jnp.bfloat16)
        up_grad = (hidden_grad * silu_gate).astype(jnp.bfloat16)
        in_grad = jnp.concatenate([gate_grad, up_grad], axis=1)
        terms = dot(in_grad, in_weight, CONTRACT_LAST).astype(jnp.bfloat16)
        return hidden, in_grad, [terms[m * seats : (m + 1) * seats] for m in range(groups)]

    def collect(seat, got):
        return dot(seat.reshape(groups * seats, row_count), jnp.concatenate(got, axis=0), CONTRACT_FIRST)

    def back(total):
        return step_on(total.astype(jnp.bfloat16), "dp", 1).astype(jnp.float32)

    seat0, sent0 = spread(rows)
    rows1 = step_on(rows, "dp", 1)
    got0 = exchange(sent0, "expert")
    rows1, got0 = lax.optimization_barrier((rows1, got0))

    rows2 = step_on(rows1, "dp", 1)
    seat1, sent1 = spread(rows1)
    got1 = exchange(sent1, "expert")
    slots0 = jnp.concatenate(got0, axis=0)
    ahead = jnp.pad(notes, ((0, groups * seats - row_count), (0, 0)))
    ahead = jnp.concatenate([slots0, ahead], axis=1)
    hidden0, in_grad0, terms0 = work(slots0)
    rows2, got1, ahead, terms0 = lax.optimization_barrier((rows2, got1, ahead, terms0))

    ahead = step_on(ahead, "dp", -1)
    seat2, sent2 = spread(rows2)
    got2 = exchange(sent2, "expert")
    slots1 = jnp.concatenate(got1, axis=0)
    hidden1, in_grad1, terms1 = work(slots1)
    got2, terms1 = lax.optimization_barrier((got2, terms1))

    back1 = exchange(terms1, "expert")
    slots2 = jnp.concatenate(got2, axis=0)
    hidden2, in_grad2, terms2 = work(slots2)
    back1, terms2, terms0 = lax.optimization_barrier((back1, terms2, terms0))
    back2 = exchange(terms2, "expert")
    passed = back(collect(seat1, back1))
    back2, ahead = lax.optimization_barrier((back2, ahead))

    back0 = exchange(terms0, "expert")
    passed = back(passed + collect(seat2, back2))
    seat3 = seating(ahead)
    slots3 = ahead[:, : 2 * model_width]
    hidden3, in_grad3, terms3 = work(slots3)
    back3 = exchange(terms3, "expert")
    passed = back(passed + collect(seat3, back3))
    total = passed + collect(seat0, back0)
    own = total.astype(jnp.bfloat16)
    halves = [own] + [flip(own, "shadow", m) for m in range(1, cores)]
    half_of = position % cores
    place = jnp.concatenate(
        [
            ((position // cores)[:, None] == row_ids[None, :]) & (half_of == core ^ m)[:, None]
            for m in range(cores)
        ],
        axis=1,
    ).astype(jnp.bfloat16)
    token_grad = select(place, jnp.concatenate(halves, axis=0))

    slot_rows = [slots0, slots1, slots2, slots3]
    hiddens = [hidden0, hidden1, hidden2, hidden3]
    in_grads = [in_grad0, in_grad1, in_grad2, in_grad3]

    slots = jnp.concatenate(slot_rows, axis=0)
    hidden = jnp.concatenate(hiddens, axis=0)
    in_grad = jnp.concatenate(in_grads, axis=0)
    in_sums = dot(slots[:, :model_width], in_grad, CONTRACT_FIRST)
    down_sums = dot(hidden, slots[:, model_width:], CONTRACT_FIRST)

    def own_units(parts):
        total = parts[0]
        for m in range(1, cores):
            total = total + flip(parts[m].astype(jnp.bfloat16), "shadow", m).astype(jnp.float32)
        return total.astype(jnp.bfloat16)[None]

    def units(start):
        return slice(start * unit_count, (start + 1) * unit_count)

    grad_gate = own_units([in_sums[:, units(m)] for m in range(cores)])
    grad_up = own_units([in_sums[:, units(cores + m)] for m in range(cores)])
    grad_down = own_units([down_sums[units(m)] for m in range(cores)])
    return (token_grad, grad_gate, grad_up, grad_down)


def solution(mesh):
    placed = (
        P(("expert", "dp"), None),
        P(("expert", "dp"), None),
        P(("expert", "dp"), None),
        P(("expert", "dp"), None),
        P("expert", None, ("dp", "shadow")),
        P("expert", None, ("dp", "shadow")),
        P("expert", ("dp", "shadow"), None),
    )
    return jax.shard_map(
        on_device,
        mesh=mesh,
        in_specs=placed,
        out_specs=(
            P(("expert", "dp"), None),
            P("expert", None, ("dp", "shadow")),
            P("expert", None, ("dp", "shadow")),
            P("expert", ("dp", "shadow"), None),
        ),
        check_vma=False,
    )
```

```python
import jax
import jax.numpy as jnp
from jax import lax
from jax.sharding import PartitionSpec as P

CONTRACT_LAST = (((1,), (1,)), ((), ()))
CONTRACT_FIRST = (((0,), (0,)), ((), ()))
MOST_PERMUTES = 8
LANES = 128


def dot(a, b, dims=(((1,), (0,)), ((), ()))):
    return lax.dot_general(a, b, dims, preferred_element_type=jnp.float32)


def select(one_hot, rows):
    return dot(one_hot, rows).astype(jnp.bfloat16)


def flip(value, axis, mask):
    size = lax.axis_size(axis)
    return lax.ppermute(value, axis, [(i, i ^ mask) for i in range(size)])


def step_on(value, axis, step):
    size = lax.axis_size(axis)
    return lax.ppermute(value, axis, [(i, (i + step) % size) for i in range(size)])


def by_permutes(axis):
    size = lax.axis_size(axis)
    return size & (size - 1) == 0 and size <= MOST_PERMUTES


def peers_of(axis):
    size = lax.axis_size(axis)
    order = jnp.arange(size, dtype=jnp.int32)
    if by_permutes(axis):
        return order ^ lax.axis_index(axis)
    return order


def exchange(parts, axis):
    if by_permutes(axis):
        return [parts[0]] + [flip(parts[m], axis, m) for m in range(1, len(parts))]
    got = lax.all_to_all(jnp.stack(parts), axis, split_axis=0, concat_axis=0, tiled=True)
    return [got[m] for m in range(len(parts))]


def on_device(tokens, expert_ids, gate_values, cotangent, w_gate, w_up, w_down):
    token_count, model_width = tokens.shape
    groups = lax.axis_size("expert")
    dp_count = lax.axis_size("dp")
    cores = lax.axis_size("shadow")
    experts = w_gate.shape[0] * groups
    capacity = max(2, 2 * token_count // experts)
    seats = -(-capacity // cores)
    row_count = token_count // cores
    unit_count = w_gate.shape[2]
    chip_units = cores * unit_count
    core = lax.axis_index("shadow")

    in_window = expert_ids < experts
    window_expert = jnp.sum(jnp.where(in_window, expert_ids, 0), axis=1)
    route_gate = jnp.sum(jnp.where(in_window, gate_values, 0.0), axis=1)
    key = window_expert * token_count + jnp.arange(token_count, dtype=jnp.int32)
    position = jnp.sum((key[None, :] < key[:, None]).astype(jnp.int32), axis=1)
    first = jnp.sum(
        (window_expert[None, :] < jnp.arange(experts + 1, dtype=jnp.int32)[:, None]).astype(jnp.int32),
        axis=1,
    )
    first_row = (first - core + cores - 1) // cores
    scaled = (route_gate[:, None] * cotangent.astype(jnp.float32)).astype(jnp.bfloat16)
    row_ids = jnp.arange(row_count, dtype=jnp.int32)
    pick = (position[None, :] == (cores * row_ids + core)[:, None]).astype(jnp.bfloat16)
    here = (first_row[:-1, None] <= row_ids) & (row_ids < first_row[1:, None])
    row_expert = jnp.sum(jnp.where(here, jnp.arange(experts, dtype=jnp.int32)[:, None], 0), axis=0)
    row_rank = row_ids - jnp.sum(jnp.where(here, first_row[:-1, None], 0), axis=0)
    notes = jnp.concatenate([row_expert, row_rank]).astype(jnp.bfloat16)
    notes = jnp.pad(notes, (0, -2 * row_count % LANES))
    noted = notes.shape[0]

    def with_notes(block):
        return jnp.concatenate([block, jnp.pad(notes[None], ((0, block.shape[0] - 1), (0, 0)))], axis=1)

    rows = with_notes(jnp.concatenate([select(pick, tokens), select(pick, scaled)], axis=1))

    peers = peers_of("expert")
    seat_ids = jnp.arange(seats, dtype=jnp.int32)

    def seating(block):
        notes = block[0, -noted:].astype(jnp.int32)
        expert, rank = notes[:row_count], notes[row_count : 2 * row_count]
        taken = (expert == peers[:, None, None]) & (rank == seat_ids[None, :, None])
        return taken.astype(jnp.bfloat16)

    def spread(block):
        seat = seating(block)
        wide = block[:, : 2 * model_width]
        return seat, [select(seat[m], wide) for m in range(groups)]

    def work(slots):
        slot_tokens, slot_cotan = slots[:, :model_width], slots[:, model_width:]
        pre = dot(slot_tokens, in_weight)
        gate_pre, up_pre = pre[:, :chip_units], pre[:, chip_units:]
        sigmoid_gate = jax.nn.sigmoid(gate_pre)
        silu_gate = gate_pre * sigmoid_gate
        hidden = (silu_gate * up_pre).astype(jnp.bfloat16)
        hidden_grad = dot(slot_cotan, down_weight, CONTRACT_LAST)
        gate_grad = (
            hidden_grad * up_pre * sigmoid_gate * (1.0 + gate_pre * (1.0 - sigmoid_gate))
        ).astype(jnp.bfloat16)
        up_grad = (hidden_grad * silu_gate).astype(jnp.bfloat16)
        in_grad = jnp.concatenate([gate_grad, up_grad], axis=1)
        terms = dot(in_grad, in_weight, CONTRACT_LAST).astype(jnp.bfloat16)
        return hidden, in_grad, [terms[m * seats : (m + 1) * seats] for m in range(groups)]

    def on_chip(weight):
        return [weight] + [flip(weight, "shadow", m) for m in range(1, cores)]

    def collect(seat, got):
        return dot(seat.reshape(groups * seats, row_count), jnp.concatenate(got, axis=0), CONTRACT_FIRST)

    def back(total, step):
        return step_on(total.astype(jnp.bfloat16), "dp", step).astype(jnp.float32)

    tie = lax.optimization_barrier
    gate_all, up_all, down_all = on_chip(w_gate[0]), on_chip(w_up[0]), on_chip(w_down[0])
    rows, gate_all, up_all, down_all = tie((rows, gate_all, up_all, down_all))
    rows1 = step_on(rows, "dp", 1)
    seat0, sent0 = spread(rows)
    got0 = exchange(sent0, "expert")
    rows1, got0[1:-1] = tie((rows1, got0[1:-1]))

    rows2 = step_on(rows1, "dp", 1)
    seat1, sent1 = spread(rows1)
    got1 = exchange(sent1, "expert")
    got1[1], got0, gate_all, up_all, down_all = tie((got1[1], got0, gate_all, up_all, down_all))
    in_weight = jnp.concatenate(gate_all + up_all, axis=1)
    down_weight = jnp.concatenate(down_all, axis=0)
    slots0 = jnp.concatenate(got0, axis=0)
    ahead = with_notes(slots0)
    rows2, got1[1:-1], ahead, in_weight, down_weight = tie((rows2, got1[1:-1], ahead, in_weight, down_weight))

    ahead = step_on(ahead, "dp", -1)
    seat2, sent2 = spread(rows2)
    got2 = exchange(sent2, "expert")
    got2[1], got1, slots0 = tie((got2[1], got1, slots0))
    slots1 = jnp.concatenate(got1, axis=0)
    hidden1, in_grad1, terms1 = work(slots1)
    hidden0, in_grad0, terms0 = work(slots0)
    got2[1:-1], terms1 = tie((got2[1:-1], terms1))

    back1 = exchange(terms1, "expert")
    back1[1], got2 = tie((back1[1], got2))
    slots2 = jnp.concatenate(got2, axis=0)
    hidden2, in_grad2, terms2 = work(slots2)
    back1[1], terms2 = tie((back1[1], terms2))
    back2 = exchange(terms2, "expert")
    back2[1], ahead, back1 = tie((back2[1], ahead, back1))

    down1 = back(collect(seat1, back1), -1)
    seat3 = seating(ahead)
    slots3 = ahead[:, : 2 * model_width]
    hidden3, in_grad3, terms3 = work(slots3)
    sum2, in_grad3 = tie((collect(seat2, back2), in_grad3))
    up2 = back(sum2, 1)
    back3 = exchange(terms3, "expert")
    back3[1], terms0 = tie((back3[1], terms0))
    sum3 = (up2 + collect(seat3, back3)).astype(jnp.bfloat16)
    up3 = step_on(sum3, "dp", 1).astype(jnp.float32)
    back0 = exchange(terms0, "expert")
    total = down1 + up3 + collect(seat0, back0)
    own = total.astype(jnp.bfloat16)

    slots = jnp.concatenate([slots0, slots1, slots2, slots3], axis=0)
    hidden = jnp.concatenate([hidden0, hidden1, hidden2, hidden3], axis=0)
    in_grad = jnp.concatenate([in_grad0, in_grad1, in_grad2, in_grad3], axis=0)
    in_sums = dot(slots[:, :model_width], in_grad, CONTRACT_FIRST)
    down_sums = dot(hidden, slots[:, model_width:], CONTRACT_FIRST)

    def own_units(parts):
        total = parts[0]
        for m in range(1, cores):
            total = total + flip(parts[m].astype(jnp.bfloat16), "shadow", m).astype(jnp.float32)
        return total.astype(jnp.bfloat16)[None]

    def units(start):
        return slice(start * unit_count, (start + 1) * unit_count)

    grad_gate = own_units([in_sums[:, units(m)] for m in range(cores)])
    grad_up = own_units([in_sums[:, units(cores + m)] for m in range(cores)])
    grad_down = own_units([down_sums[units(m)] for m in range(cores)])
    own, grad_gate, grad_up, grad_down = tie((own, grad_gate, grad_up, grad_down))

    halves = [own] + [flip(own, "shadow", m) for m in range(1, cores)]
    half_of = position % cores
    place = jnp.concatenate(
        [
            ((position // cores)[:, None] == row_ids[None, :]) & (half_of == core ^ m)[:, None]
            for m in range(cores)
        ],
        axis=1,
    ).astype(jnp.bfloat16)
    token_grad = select(place, jnp.concatenate(halves, axis=0))

    return (token_grad, grad_gate, grad_up, grad_down)


def solution(mesh):
    placed = (
        P(("expert", "dp"), None),
        P(("expert", "dp"), None),
        P(("expert", "dp"), None),
        P(("expert", "dp"), None),
        P("expert", None, ("dp", "shadow")),
        P("expert", None, ("dp", "shadow")),
        P("expert", ("dp", "shadow"), None),
    )
    return jax.shard_map(
        on_device,
        mesh=mesh,
        in_specs=placed,
        out_specs=(
            P(("expert", "dp"), None),
            P("expert", None, ("dp", "shadow")),
            P("expert", None, ("dp", "shadow")),
            P("expert", ("dp", "shadow"), None),
        ),
        check_vma=False,
    )
```

```python
import functools

import jax
import jax.numpy as jnp
from jax import lax
from jax.experimental import pallas as pl
from jax.experimental.pallas import tpu as pltpu
from jax.sharding import PartitionSpec as P

CONTRACT_LAST = (((1,), (1,)), ((), ()))
CONTRACT_FIRST = (((0,), (0,)), ((), ()))
MOST_PERMUTES = 8
LANES = 128
STEPS = 7
VMEM_BYTES = 10 * 1024 * 1024


def dot(a, b, dims=(((1,), (0,)), ((), ()))):
    return lax.dot_general(a, b, dims, preferred_element_type=jnp.float32)


def select(one_hot, rows):
    return dot(one_hot, rows).astype(jnp.bfloat16)


def flip(value, axis, mask):
    size = lax.axis_size(axis)
    return lax.ppermute(value, axis, [(i, i ^ mask) for i in range(size)])


def step_on(value, axis, step):
    size = lax.axis_size(axis)
    return lax.ppermute(value, axis, [(i, (i + step) % size) for i in range(size)])


def by_permutes(axis):
    size = lax.axis_size(axis)
    return size & (size - 1) == 0 and size <= MOST_PERMUTES


def peers_of(axis):
    size = lax.axis_size(axis)
    order = jnp.arange(size, dtype=jnp.int32)
    if by_permutes(axis):
        return order ^ lax.axis_index(axis)
    return order


def exchange(parts, axis):
    if by_permutes(axis):
        return [parts[0]] + [flip(parts[m], axis, m) for m in range(1, len(parts))]
    got = lax.all_to_all(jnp.stack(parts), axis, split_axis=0, concat_axis=0, tiled=True)
    return [got[m] for m in range(len(parts))]


def expert_pass(groups, *refs):
    piece_refs, (in_weight_ref, down_weight_ref) = refs[:groups], refs[groups : groups + 2]
    slots_ref, hidden_ref, in_grad_ref = refs[groups + 2 : groups + 5]
    terms_refs = refs[groups + 5 :]
    seats = terms_refs[0].shape[0]
    held = piece_refs[0].shape[0]
    width, units = in_weight_ref.shape[0], down_weight_ref.shape[0]
    for m, piece_ref in enumerate(piece_refs):
        slots_ref[m * held : (m + 1) * held] = piece_ref[:, : 2 * width]
    step = width // STEPS
    spans = [slice(at * step, (at + 1) * step) for at in range(STEPS)]
    pre = hidden_grad = 0.0
    for span in spans:
        beyond = slice(width + span.start, width + span.stop)
        pre += dot(slots_ref[:, span], in_weight_ref[span])
        hidden_grad += dot(slots_ref[:, beyond], down_weight_ref[:, span], CONTRACT_LAST)
    gate_pre, up_pre = pre[:, :units], pre[:, units:]
    sigmoid_gate = jax.nn.sigmoid(gate_pre)
    silu_gate = gate_pre * sigmoid_gate
    hidden_ref[...] = (silu_gate * up_pre).astype(jnp.bfloat16)
    in_grad_ref[:, :units] = (
        hidden_grad * up_pre * sigmoid_gate * (1.0 + gate_pre * (1.0 - sigmoid_gate))
    ).astype(jnp.bfloat16)
    in_grad_ref[:, units:] = (hidden_grad * silu_gate).astype(jnp.bfloat16)
    in_grad = in_grad_ref[...]
    for span in spans:
        terms = dot(in_grad, in_weight_ref[span], CONTRACT_LAST).astype(jnp.bfloat16)
        for m, terms_ref in enumerate(terms_refs):
            terms_ref[:, span] = terms[m * seats : (m + 1) * seats]


def on_device(tokens, expert_ids, gate_values, cotangent, w_gate, w_up, w_down):
    token_count, model_width = tokens.shape
    groups = lax.axis_size("expert")
    dp_count = lax.axis_size("dp")
    cores = lax.axis_size("shadow")
    experts = w_gate.shape[0] * groups
    capacity = max(2, 2 * token_count // experts)
    seats = -(-capacity // cores)
    row_count = token_count // cores
    unit_count = w_gate.shape[2]
    chip_units = cores * unit_count
    core = lax.axis_index("shadow")

    in_window = expert_ids < experts
    window_expert = jnp.sum(jnp.where(in_window, expert_ids, 0), axis=1)
    route_gate = jnp.sum(jnp.where(in_window, gate_values, 0.0), axis=1)
    key = window_expert * token_count + jnp.arange(token_count, dtype=jnp.int32)
    position = jnp.sum((key[None, :] < key[:, None]).astype(jnp.int32), axis=1)
    first = jnp.sum(
        (window_expert[None, :] < jnp.arange(experts + 1, dtype=jnp.int32)[:, None]).astype(jnp.int32),
        axis=1,
    )
    first_row = (first - core + cores - 1) // cores
    scaled = (route_gate[:, None] * cotangent.astype(jnp.float32)).astype(jnp.bfloat16)
    row_ids = jnp.arange(row_count, dtype=jnp.int32)
    pick = (position[None, :] == (cores * row_ids + core)[:, None]).astype(jnp.bfloat16)
    here = (first_row[:-1, None] <= row_ids) & (row_ids < first_row[1:, None])
    row_expert = jnp.sum(jnp.where(here, jnp.arange(experts, dtype=jnp.int32)[:, None], 0), axis=0)
    row_rank = row_ids - jnp.sum(jnp.where(here, first_row[:-1, None], 0), axis=0)
    notes = jnp.concatenate([row_expert, row_rank]).astype(jnp.bfloat16)
    notes = jnp.pad(notes, (0, -2 * row_count % LANES))
    noted = notes.shape[0]

    def with_notes(block):
        return jnp.concatenate([block, jnp.pad(notes[None], ((0, block.shape[0] - 1), (0, 0)))], axis=1)

    rows = with_notes(jnp.concatenate([select(pick, tokens), select(pick, scaled)], axis=1))

    peers = peers_of("expert")
    seat_ids = jnp.arange(seats, dtype=jnp.int32)

    def seating(block):
        notes = block[0, -noted:].astype(jnp.int32)
        expert, rank = notes[:row_count], notes[row_count : 2 * row_count]
        taken = (expert == peers[:, None, None]) & (rank == seat_ids[None, :, None])
        return taken.astype(jnp.bfloat16)

    def spread(block):
        seat = seating(block)
        wide = block[:, : 2 * model_width]
        return seat, [select(seat[m], wide) for m in range(groups)]

    def work(pieces):
        whole = pl.BlockSpec(memory_space=pltpu.VMEM)
        slot_count = groups * seats
        shape = functools.partial(jax.ShapeDtypeStruct, dtype=jnp.bfloat16)
        slots, hidden, in_grad, *terms = pl.pallas_call(
            functools.partial(expert_pass, len(pieces)),
            out_shape=[
                shape((slot_count, 2 * model_width)),
                shape((slot_count, chip_units)),
                shape((slot_count, 2 * chip_units)),
            ]
            + [shape((seats, model_width))] * groups,
            in_specs=[whole] * (len(pieces) + 2),
            out_specs=[whole] * (3 + groups),
            compiler_params=pltpu.CompilerParams(vmem_limit_bytes=VMEM_BYTES),
            cost_estimate=pl.CostEstimate(flops=0, bytes_accessed=0, transcendentals=0),
            name="expert_pass",
        )(*pieces, in_weight, down_weight)
        return slots, hidden, in_grad, terms

    def on_chip(weight):
        return [weight] + [flip(weight, "shadow", m) for m in range(1, cores)]

    def collect(seat, got):
        return dot(seat.reshape(groups * seats, row_count), jnp.concatenate(got, axis=0), CONTRACT_FIRST)

    def back(total, step):
        return step_on(total.astype(jnp.bfloat16), "dp", step).astype(jnp.float32)

    tie = lax.optimization_barrier
    gate_all, up_all, down_all = on_chip(w_gate[0]), on_chip(w_up[0]), on_chip(w_down[0])
    rows, gate_all, up_all, down_all = tie((rows, gate_all, up_all, down_all))
    rows1 = step_on(rows, "dp", 1)
    seat0, sent0 = spread(rows)
    got0 = exchange(sent0, "expert")
    rows1, got0[1] = tie((rows1, got0[1]))
    rows2 = step_on(rows1, "dp", 1)
    rows1, got0[1:-1] = tie((rows1, got0[1:-1]))

    seat1, sent1 = spread(rows1)
    got1 = exchange(sent1, "expert")
    got1[1], got0, gate_all, up_all, down_all = tie((got1[1], got0, gate_all, up_all, down_all))
    in_weight = jnp.concatenate(gate_all + up_all, axis=1)
    down_weight = jnp.concatenate(down_all, axis=0)
    ahead0 = jnp.concatenate(got0, axis=0)
    ahead = with_notes(ahead0)
    rows2, ahead, in_weight, down_weight = tie((rows2, ahead, in_weight, down_weight))
    ahead = step_on(ahead, "dp", -1)
    rows2, got1[1:-1] = tie((rows2, got1[1:-1]))

    seat2, sent2 = spread(rows2)
    got2 = exchange(sent2, "expert")
    got2[1], got1, got0 = tie((got2[1], got1, got0))
    slots1, hidden1, in_grad1, terms1 = work(got1)
    slots0, hidden0, in_grad0, terms0 = work(got0)
    got2[1:-1], terms1 = tie((got2[1:-1], terms1))

    back1 = exchange(terms1, "expert")
    back1[1], got2 = tie((back1[1], got2))
    slots2, hidden2, in_grad2, terms2 = work(got2)
    back1[1], terms2 = tie((back1[1], terms2))
    back2 = exchange(terms2, "expert")
    back2[1], ahead, back1 = tie((back2[1], ahead, back1))

    down1 = back(collect(seat1, back1), -1)
    seat3 = seating(ahead)
    slots3, hidden3, in_grad3, terms3 = work([ahead])
    sum2, in_grad3 = tie((collect(seat2, back2), in_grad3))
    up2 = back(sum2, 1)
    back3 = exchange(terms3, "expert")
    back3[1], terms0 = tie((back3[1], terms0))
    sum3 = (up2 + collect(seat3, back3)).astype(jnp.bfloat16)
    up3 = step_on(sum3, "dp", 1).astype(jnp.float32)
    back0 = exchange(terms0, "expert")
    total = down1 + up3 + collect(seat0, back0)
    own = total.astype(jnp.bfloat16)

    slots = jnp.concatenate([slots0, slots1, slots2, slots3], axis=0)
    hidden = jnp.concatenate([hidden0, hidden1, hidden2, hidden3], axis=0)
    in_grad = jnp.concatenate([in_grad0, in_grad1, in_grad2, in_grad3], axis=0)
    in_sums = dot(slots[:, :model_width], in_grad, CONTRACT_FIRST)
    down_sums = dot(hidden, slots[:, model_width:], CONTRACT_FIRST)

    def own_units(parts):
        total = parts[0]
        for m in range(1, cores):
            total = total + flip(parts[m].astype(jnp.bfloat16), "shadow", m).astype(jnp.float32)
        return total.astype(jnp.bfloat16)[None]

    def units(start):
        return slice(start * unit_count, (start + 1) * unit_count)

    grad_gate = own_units([in_sums[:, units(m)] for m in range(cores)])
    grad_up = own_units([in_sums[:, units(cores + m)] for m in range(cores)])
    grad_down = own_units([down_sums[units(m)] for m in range(cores)])
    own, grad_gate, grad_up, grad_down = tie((own, grad_gate, grad_up, grad_down))

    halves = [own] + [flip(own, "shadow", m) for m in range(1, cores)]
    half_of = position % cores
    place = jnp.concatenate(
        [
            ((position // cores)[:, None] == row_ids[None, :]) & (half_of == core ^ m)[:, None]
            for m in range(cores)
        ],
        axis=1,
    ).astype(jnp.bfloat16)
    token_grad = select(place, jnp.concatenate(halves, axis=0))

    return (token_grad, grad_gate, grad_up, grad_down)


def solution(mesh):
    placed = (
        P(("expert", "dp"), None),
        P(("expert", "dp"), None),
        P(("expert", "dp"), None),
        P(("expert", "dp"), None),
        P("expert", None, ("dp", "shadow")),
        P("expert", None, ("dp", "shadow")),
        P("expert", ("dp", "shadow"), None),
    )
    return jax.shard_map(
        on_device,
        mesh=mesh,
        in_specs=placed,
        out_specs=(
            P(("expert", "dp"), None),
            P("expert", None, ("dp", "shadow")),
            P("expert", None, ("dp", "shadow")),
            P("expert", ("dp", "shadow"), None),
        ),
        check_vma=False,
    )
```

```python
import functools

import jax
import jax.numpy as jnp
from jax import lax
from jax.experimental import pallas as pl
from jax.experimental.pallas import tpu as pltpu
from jax.sharding import PartitionSpec as P

CONTRACT_LAST = (((1,), (1,)), ((), ()))
CONTRACT_FIRST = (((0,), (0,)), ((), ()))
MOST_PERMUTES = 8
LANES = 128
STEPS = 7
VMEM_BYTES = 10 * 1024 * 1024


def dot(a, b, dims=(((1,), (0,)), ((), ()))):
    return lax.dot_general(a, b, dims, preferred_element_type=jnp.float32)


def select(one_hot, rows):
    return dot(one_hot, rows).astype(jnp.bfloat16)


def flip(value, axis, mask):
    size = lax.axis_size(axis)
    return lax.ppermute(value, axis, [(i, i ^ mask) for i in range(size)])


def step_on(value, axis, step):
    size = lax.axis_size(axis)
    return lax.ppermute(value, axis, [(i, (i + step) % size) for i in range(size)])


def by_permutes(axis):
    size = lax.axis_size(axis)
    return size & (size - 1) == 0 and size <= MOST_PERMUTES


def peers_of(axis):
    size = lax.axis_size(axis)
    order = jnp.arange(size, dtype=jnp.int32)
    if by_permutes(axis):
        return order ^ lax.axis_index(axis)
    return order


def exchange(parts, axis):
    if by_permutes(axis):
        return [parts[0]] + [flip(parts[m], axis, m) for m in range(1, len(parts))]
    got = lax.all_to_all(jnp.stack(parts), axis, split_axis=0, concat_axis=0, tiled=True)
    return [got[m] for m in range(len(parts))]


def expert_pass(groups, *refs):
    piece_refs, (in_weight_ref, down_weight_ref) = refs[:groups], refs[groups : groups + 2]
    slots_ref, hidden_ref, in_grad_ref = refs[groups + 2 : groups + 5]
    terms_refs = refs[groups + 5 :]
    seats = terms_refs[0].shape[0]
    held = piece_refs[0].shape[0]
    width, units = in_weight_ref.shape[0], down_weight_ref.shape[0]
    for m, piece_ref in enumerate(piece_refs):
        slots_ref[m * held : (m + 1) * held] = piece_ref[:, : 2 * width]
    step = width // STEPS
    spans = [slice(at * step, (at + 1) * step) for at in range(STEPS)]
    pre = hidden_grad = 0.0
    for span in spans:
        beyond = slice(width + span.start, width + span.stop)
        pre += dot(slots_ref[:, span], in_weight_ref[span])
        hidden_grad += dot(slots_ref[:, beyond], down_weight_ref[:, span], CONTRACT_LAST)
    gate_pre, up_pre = pre[:, :units], pre[:, units:]
    sigmoid_gate = jax.nn.sigmoid(gate_pre)
    silu_gate = gate_pre * sigmoid_gate
    hidden_ref[...] = (silu_gate * up_pre).astype(jnp.bfloat16)
    in_grad_ref[:, :units] = (
        hidden_grad * up_pre * sigmoid_gate * (1.0 + gate_pre * (1.0 - sigmoid_gate))
    ).astype(jnp.bfloat16)
    in_grad_ref[:, units:] = (hidden_grad * silu_gate).astype(jnp.bfloat16)
    in_grad = in_grad_ref[...]
    for span in spans:
        terms = dot(in_grad, in_weight_ref[span], CONTRACT_LAST).astype(jnp.bfloat16)
        for m, terms_ref in enumerate(terms_refs):
            terms_ref[:, span] = terms[m * seats : (m + 1) * seats]


def on_device(tokens, expert_ids, gate_values, cotangent, w_gate, w_up, w_down):
    token_count, model_width = tokens.shape
    groups = lax.axis_size("expert")
    dp_count = lax.axis_size("dp")
    cores = lax.axis_size("shadow")
    experts = w_gate.shape[0] * groups
    capacity = max(2, 2 * token_count // experts)
    seats = -(-capacity // cores)
    row_count = token_count // cores
    unit_count = w_gate.shape[2]
    chip_units = cores * unit_count
    core = lax.axis_index("shadow")

    in_window = expert_ids < experts
    window_expert = jnp.sum(jnp.where(in_window, expert_ids, 0), axis=1)
    route_gate = jnp.sum(jnp.where(in_window, gate_values, 0.0), axis=1)
    key = window_expert * token_count + jnp.arange(token_count, dtype=jnp.int32)
    position = jnp.sum((key[None, :] < key[:, None]).astype(jnp.int32), axis=1)
    first = jnp.sum(
        (window_expert[None, :] < jnp.arange(experts + 1, dtype=jnp.int32)[:, None]).astype(jnp.int32),
        axis=1,
    )
    first_row = (first - core + cores - 1) // cores
    scaled = (route_gate[:, None] * cotangent.astype(jnp.float32)).astype(jnp.bfloat16)
    row_ids = jnp.arange(row_count, dtype=jnp.int32)
    pick = (position[None, :] == (cores * row_ids + core)[:, None]).astype(jnp.bfloat16)
    here = (first_row[:-1, None] <= row_ids) & (row_ids < first_row[1:, None])
    row_expert = jnp.sum(jnp.where(here, jnp.arange(experts, dtype=jnp.int32)[:, None], 0), axis=0)
    row_rank = row_ids - jnp.sum(jnp.where(here, first_row[:-1, None], 0), axis=0)
    notes = jnp.concatenate([row_expert, row_rank]).astype(jnp.bfloat16)
    notes = jnp.pad(notes, (0, -2 * row_count % LANES))
    noted = notes.shape[0]

    def with_notes(block):
        return jnp.concatenate([block, jnp.pad(notes[None], ((0, block.shape[0] - 1), (0, 0)))], axis=1)

    rows = with_notes(jnp.concatenate([select(pick, tokens), select(pick, scaled)], axis=1))

    peers = peers_of("expert")
    seat_ids = jnp.arange(seats, dtype=jnp.int32)

    def seating(block):
        notes = block[0, -noted:].astype(jnp.int32)
        expert, rank = notes[:row_count], notes[row_count : 2 * row_count]
        taken = (expert == peers[:, None, None]) & (rank == seat_ids[None, :, None])
        return taken.astype(jnp.bfloat16)

    def spread(block):
        seat = seating(block)
        wide = block[:, : 2 * model_width]
        return seat, [select(seat[m], wide) for m in range(groups)]

    def work(pieces):
        whole = pl.BlockSpec(memory_space=pltpu.VMEM)
        slot_count = groups * seats
        shape = functools.partial(jax.ShapeDtypeStruct, dtype=jnp.bfloat16)
        slots, hidden, in_grad, *terms = pl.pallas_call(
            functools.partial(expert_pass, len(pieces)),
            out_shape=[
                shape((slot_count, 2 * model_width)),
                shape((slot_count, chip_units)),
                shape((slot_count, 2 * chip_units)),
            ]
            + [shape((seats, model_width))] * groups,
            in_specs=[whole] * (len(pieces) + 2),
            out_specs=[whole] * (3 + groups),
            compiler_params=pltpu.CompilerParams(vmem_limit_bytes=VMEM_BYTES),
            cost_estimate=pl.CostEstimate(flops=0, bytes_accessed=0, transcendentals=0),
            name="expert_pass",
        )(*pieces, in_weight, down_weight)
        return slots, hidden, in_grad, terms

    def on_chip(weight):
        return [weight] + [flip(weight, "shadow", m) for m in range(1, cores)]

    def collect(seat, got):
        return dot(seat.reshape(groups * seats, row_count), jnp.concatenate(got, axis=0), CONTRACT_FIRST)

    def back(total, step):
        return step_on(total.astype(jnp.bfloat16), "dp", step).astype(jnp.float32)

    tie = lax.optimization_barrier
    gate_all, up_all, down_all = on_chip(w_gate[0]), on_chip(w_up[0]), on_chip(w_down[0])
    rows, gate_all, up_all, down_all = tie((rows, gate_all, up_all, down_all))
    rows1 = step_on(rows, "dp", 1)
    seat0, sent0 = spread(rows)
    got0 = exchange(sent0, "expert")
    rows1, got0[1] = tie((rows1, got0[1]))
    rows2 = step_on(rows1, "dp", 1)
    rows1, got0[1:-1] = tie((rows1, got0[1:-1]))

    seat1, sent1 = spread(rows1)
    got1 = exchange(sent1, "expert")
    got1[1], got0, gate_all, up_all, down_all = tie((got1[1], got0, gate_all, up_all, down_all))
    in_weight = jnp.concatenate(gate_all + up_all, axis=1)
    down_weight = jnp.concatenate(down_all, axis=0)
    ahead0 = jnp.concatenate(got0, axis=0)
    ahead = with_notes(ahead0)
    ahead = step_on(ahead, "dp", -1)
    rows2, got1[1:], in_weight, down_weight = tie((rows2, got1[1:], in_weight, down_weight))

    seat2, sent2 = spread(rows2)
    got2 = exchange(sent2, "expert")
    got2[1], got1, got0 = tie((got2[1], got1, got0))
    slots1, hidden1, in_grad1, terms1 = work(got1)
    slots0, hidden0, in_grad0, terms0 = work(got0)
    got2[1:-1], terms1 = tie((got2[1:-1], terms1))

    back1 = exchange(terms1, "expert")
    back1[1], got2 = tie((back1[1], got2))
    slots2, hidden2, in_grad2, terms2 = work(got2)
    back1[1], terms2 = tie((back1[1], terms2))
    back2 = exchange(terms2, "expert")
    back2[1], ahead, back1 = tie((back2[1], ahead, back1))

    down1 = back(collect(seat1, back1), -1)
    seat3 = seating(ahead)
    slots3, hidden3, in_grad3, terms3 = work([ahead])
    up2 = back(collect(seat2, back2), 1)
    back3 = exchange(terms3, "expert")
    back3[1], terms0 = tie((back3[1], terms0))
    sum3 = (up2 + collect(seat3, back3)).astype(jnp.bfloat16)
    up3 = step_on(sum3, "dp", 1).astype(jnp.float32)
    back0 = exchange(terms0, "expert")
    back0[1], in_grad3, slots3 = tie((back0[1], in_grad3, slots3))
    total = down1 + up3 + collect(seat0, back0)
    own = total.astype(jnp.bfloat16)

    slots = jnp.concatenate([slots0, slots1, slots2, slots3], axis=0)
    hidden = jnp.concatenate([hidden0, hidden1, hidden2, hidden3], axis=0)
    in_grad = jnp.concatenate([in_grad0, in_grad1, in_grad2, in_grad3], axis=0)
    in_sums = dot(slots[:, :model_width], in_grad, CONTRACT_FIRST)
    down_sums = dot(hidden, slots[:, model_width:], CONTRACT_FIRST)

    def own_units(parts):
        total = parts[0]
        for m in range(1, cores):
            total = total + flip(parts[m].astype(jnp.bfloat16), "shadow", m).astype(jnp.float32)
        return total.astype(jnp.bfloat16)[None]

    def units(start):
        return slice(start * unit_count, (start + 1) * unit_count)

    grad_gate = own_units([in_sums[:, units(m)] for m in range(cores)])
    grad_up = own_units([in_sums[:, units(cores + m)] for m in range(cores)])
    grad_down = own_units([down_sums[units(m)] for m in range(cores)])
    own, grad_gate, grad_up, grad_down = tie((own, grad_gate, grad_up, grad_down))

    halves = [own] + [flip(own, "shadow", m) for m in range(1, cores)]
    half_of = position % cores
    place = jnp.concatenate(
        [
            ((position // cores)[:, None] == row_ids[None, :]) & (half_of == core ^ m)[:, None]
            for m in range(cores)
        ],
        axis=1,
    ).astype(jnp.bfloat16)
    token_grad = select(place, jnp.concatenate(halves, axis=0))

    return (token_grad, grad_gate, grad_up, grad_down)


def solution(mesh):
    placed = (
        P(("expert", "dp"), None),
        P(("expert", "dp"), None),
        P(("expert", "dp"), None),
        P(("expert", "dp"), None),
        P("expert", None, ("dp", "shadow")),
        P("expert", None, ("dp", "shadow")),
        P("expert", ("dp", "shadow"), None),
    )
    return jax.shard_map(
        on_device,
        mesh=mesh,
        in_specs=placed,
        out_specs=(
            P(("expert", "dp"), None),
            P("expert", None, ("dp", "shadow")),
            P("expert", None, ("dp", "shadow")),
            P("expert", ("dp", "shadow"), None),
        ),
        check_vma=False,
    )
```

```python
import functools

import jax
import jax.numpy as jnp
from jax import lax
from jax.experimental import pallas as pl
from jax.experimental.pallas import tpu as pltpu
from jax.sharding import PartitionSpec as P

CONTRACT_LAST = (((1,), (1,)), ((), ()))
CONTRACT_FIRST = (((0,), (0,)), ((), ()))
MOST_PERMUTES = 8
LANES = 128
STEPS = 7
VMEM_BYTES = 10 * 1024 * 1024


def dot(a, b, dims=(((1,), (0,)), ((), ()))):
    return lax.dot_general(a, b, dims, preferred_element_type=jnp.float32)


def select(one_hot, rows):
    return dot(one_hot, rows).astype(jnp.bfloat16)


def flip(value, axis, mask):
    size = lax.axis_size(axis)
    return lax.ppermute(value, axis, [(i, i ^ mask) for i in range(size)])


def step_on(value, axis, step):
    size = lax.axis_size(axis)
    return lax.ppermute(value, axis, [(i, (i + step) % size) for i in range(size)])


def by_permutes(axis):
    size = lax.axis_size(axis)
    return size & (size - 1) == 0 and size <= MOST_PERMUTES


def peers_of(axis):
    size = lax.axis_size(axis)
    order = jnp.arange(size, dtype=jnp.int32)
    if by_permutes(axis):
        return order ^ lax.axis_index(axis)
    return order


def exchange(parts, axis):
    if by_permutes(axis):
        return [parts[0]] + [flip(parts[m], axis, m) for m in range(1, len(parts))]
    got = lax.all_to_all(jnp.stack(parts), axis, split_axis=0, concat_axis=0, tiled=True)
    return [got[m] for m in range(len(parts))]


def expert_pass(groups, *refs):
    piece_refs, (in_weight_ref, down_weight_ref) = refs[:groups], refs[groups : groups + 2]
    slots_ref, hidden_ref, in_grad_ref = refs[groups + 2 : groups + 5]
    terms_refs = refs[groups + 5 :]
    seats = terms_refs[0].shape[0]
    held = piece_refs[0].shape[0]
    width, units = in_weight_ref.shape[0], down_weight_ref.shape[0]
    for m, piece_ref in enumerate(piece_refs):
        slots_ref[m * held : (m + 1) * held] = piece_ref[:, : 2 * width]
    step = width // STEPS
    spans = [slice(at * step, (at + 1) * step) for at in range(STEPS)]
    pre = hidden_grad = 0.0
    for span in spans:
        beyond = slice(width + span.start, width + span.stop)
        pre += dot(slots_ref[:, span], in_weight_ref[span])
        hidden_grad += dot(slots_ref[:, beyond], down_weight_ref[:, span], CONTRACT_LAST)
    gate_pre, up_pre = pre[:, :units], pre[:, units:]
    sigmoid_gate = jax.nn.sigmoid(gate_pre)
    silu_gate = gate_pre * sigmoid_gate
    hidden_ref[...] = (silu_gate * up_pre).astype(jnp.bfloat16)
    in_grad_ref[:, :units] = (
        hidden_grad * up_pre * sigmoid_gate * (1.0 + gate_pre * (1.0 - sigmoid_gate))
    ).astype(jnp.bfloat16)
    in_grad_ref[:, units:] = (hidden_grad * silu_gate).astype(jnp.bfloat16)
    in_grad = in_grad_ref[...]
    for span in spans:
        terms = dot(in_grad, in_weight_ref[span], CONTRACT_LAST).astype(jnp.bfloat16)
        for m, terms_ref in enumerate(terms_refs):
            terms_ref[:, span] = terms[m * seats : (m + 1) * seats]


def on_device(tokens, expert_ids, gate_values, cotangent, w_gate, w_up, w_down):
    token_count, model_width = tokens.shape
    groups = lax.axis_size("expert")
    dp_count = lax.axis_size("dp")
    cores = lax.axis_size("shadow")
    experts = w_gate.shape[0] * groups
    capacity = max(2, 2 * token_count // experts)
    seats = -(-capacity // cores)
    row_count = token_count // cores
    unit_count = w_gate.shape[2]
    chip_units = cores * unit_count
    core = lax.axis_index("shadow")

    in_window = expert_ids < experts
    window_expert = jnp.sum(jnp.where(in_window, expert_ids, 0), axis=1)
    route_gate = jnp.sum(jnp.where(in_window, gate_values, 0.0), axis=1)
    key = window_expert * token_count + jnp.arange(token_count, dtype=jnp.int32)
    position = jnp.sum((key[None, :] < key[:, None]).astype(jnp.int32), axis=1)
    first = jnp.sum(
        (window_expert[None, :] < jnp.arange(experts + 1, dtype=jnp.int32)[:, None]).astype(jnp.int32),
        axis=1,
    )
    first_row = (first - core + cores - 1) // cores
    scaled = (route_gate[:, None] * cotangent.astype(jnp.float32)).astype(jnp.bfloat16)
    row_ids = jnp.arange(row_count, dtype=jnp.int32)
    pick = (position[None, :] == (cores * row_ids + core)[:, None]).astype(jnp.bfloat16)
    here = (first_row[:-1, None] <= row_ids) & (row_ids < first_row[1:, None])
    row_expert = jnp.sum(jnp.where(here, jnp.arange(experts, dtype=jnp.int32)[:, None], 0), axis=0)
    row_rank = row_ids - jnp.sum(jnp.where(here, first_row[:-1, None], 0), axis=0)
    notes = jnp.concatenate([row_expert, row_rank]).astype(jnp.bfloat16)
    notes = jnp.pad(notes, (0, -2 * row_count % LANES))
    noted = notes.shape[0]

    def with_notes(block):
        return jnp.concatenate([block, jnp.pad(notes[None], ((0, block.shape[0] - 1), (0, 0)))], axis=1)

    rows = with_notes(jnp.concatenate([select(pick, tokens), select(pick, scaled)], axis=1))

    peers = peers_of("expert")
    seat_ids = jnp.arange(seats, dtype=jnp.int32)

    def seating(block):
        notes = block[0, -noted:].astype(jnp.int32)
        expert, rank = notes[:row_count], notes[row_count : 2 * row_count]
        taken = (expert == peers[:, None, None]) & (rank == seat_ids[None, :, None])
        return taken.astype(jnp.bfloat16)

    def spread(block):
        seat = seating(block)
        wide = block[:, : 2 * model_width]
        return seat, [select(seat[m], wide) for m in range(groups)]

    def work(pieces):
        whole = pl.BlockSpec(memory_space=pltpu.VMEM)
        slot_count = groups * seats
        shape = functools.partial(jax.ShapeDtypeStruct, dtype=jnp.bfloat16)
        slots, hidden, in_grad, *terms = pl.pallas_call(
            functools.partial(expert_pass, len(pieces)),
            out_shape=[
                shape((slot_count, 2 * model_width)),
                shape((slot_count, chip_units)),
                shape((slot_count, 2 * chip_units)),
            ]
            + [shape((seats, model_width))] * groups,
            in_specs=[whole] * (len(pieces) + 2),
            out_specs=[whole] * (3 + groups),
            compiler_params=pltpu.CompilerParams(vmem_limit_bytes=VMEM_BYTES),
            cost_estimate=pl.CostEstimate(flops=0, bytes_accessed=0, transcendentals=0),
            name="expert_pass",
        )(*pieces, in_weight, down_weight)
        return slots, hidden, in_grad, terms

    def on_chip(weight):
        return [weight] + [flip(weight, "shadow", m) for m in range(1, cores)]

    def collect(seat, got):
        return dot(seat.reshape(groups * seats, row_count), jnp.concatenate(got, axis=0), CONTRACT_FIRST)

    def back(total, step):
        return step_on(total.astype(jnp.bfloat16), "dp", step).astype(jnp.float32)

    tie = lax.optimization_barrier
    gate_all, up_all, down_all = on_chip(w_gate[0]), on_chip(w_up[0]), on_chip(w_down[0])
    rows, gate_all, up_all, down_all = tie((rows, gate_all, up_all, down_all))
    rows1 = step_on(rows, "dp", 1)
    seat0, sent0 = spread(rows)
    got0 = exchange(sent0, "expert")
    rows1, got0[1] = tie((rows1, got0[1]))
    rows2 = step_on(rows1, "dp", 1)
    rows1, got0[1:-1] = tie((rows1, got0[1:-1]))

    seat1, sent1 = spread(rows1)
    got1 = exchange(sent1, "expert")
    got1[1], got0, gate_all, up_all, down_all = tie((got1[1], got0, gate_all, up_all, down_all))
    in_weight = jnp.concatenate(gate_all + up_all, axis=1)
    down_weight = jnp.concatenate(down_all, axis=0)
    ahead0 = jnp.concatenate(got0, axis=0)
    ahead = with_notes(ahead0)
    ahead = step_on(ahead, "dp", -1)
    rows2, got1[1:], in_weight, down_weight = tie((rows2, got1[1:], in_weight, down_weight))

    seat2, sent2 = spread(rows2)
    got2 = exchange(sent2, "expert")
    got2[1], got1, got0 = tie((got2[1], got1, got0))
    slots1, hidden1, in_grad1, terms1 = work(got1)
    slots0, hidden0, in_grad0, terms0 = work(got0)
    got2[1:-1], terms1 = tie((got2[1:-1], terms1))

    back1 = exchange(terms1, "expert")
    back1[1], got2 = tie((back1[1], got2))
    slots2, hidden2, in_grad2, terms2 = work(got2)
    back1[1], terms2 = tie((back1[1], terms2))
    back2 = exchange(terms2, "expert")
    back2[1], ahead, back1 = tie((back2[1], ahead, back1))

    down1 = back(collect(seat1, back1), -1)
    seat3 = seating(ahead)
    slots3, hidden3, in_grad3, terms3 = work([ahead])
    up2 = back(collect(seat2, back2), 1)
    back3 = exchange(terms3, "expert")
    back3[1], terms0 = tie((back3[1], terms0))
    sum3 = (up2 + collect(seat3, back3)).astype(jnp.bfloat16)
    up3 = step_on(sum3, "dp", 1).astype(jnp.float32)
    back0 = exchange(terms0, "expert")
    back0[1], in_grad3, slots3 = tie((back0[1], in_grad3, slots3))
    total = down1 + up3 + collect(seat0, back0)
    own = total.astype(jnp.bfloat16)

    slots = jnp.concatenate([slots0, slots1, slots2, slots3], axis=0)
    hidden = jnp.concatenate([hidden0, hidden1, hidden2, hidden3], axis=0)
    in_grad = jnp.concatenate([in_grad0, in_grad1, in_grad2, in_grad3], axis=0)
    in_sums = dot(slots[:, :model_width], in_grad, CONTRACT_FIRST)
    down_sums = dot(hidden, slots[:, model_width:], CONTRACT_FIRST)

    def own_units(parts):
        total = parts[0]
        for m in range(1, cores):
            total = total + flip(parts[m].astype(jnp.bfloat16), "shadow", m).astype(jnp.float32)
        return total.astype(jnp.bfloat16)[None]

    def units(start):
        return slice(start * unit_count, (start + 1) * unit_count)

    grad_gate = own_units([in_sums[:, units(m)] for m in range(cores)])
    grad_up = own_units([in_sums[:, units(cores + m)] for m in range(cores)])
    grad_down = own_units([down_sums[units(m)] for m in range(cores)])
    own, grad_down = tie((own, grad_down))

    halves = [own] + [flip(own, "shadow", m) for m in range(1, cores)]
    half_of = position % cores
    place = jnp.concatenate(
        [
            ((position // cores)[:, None] == row_ids[None, :]) & (half_of == core ^ m)[:, None]
            for m in range(cores)
        ],
        axis=1,
    ).astype(jnp.bfloat16)
    token_grad = select(place, jnp.concatenate(halves, axis=0))

    return (token_grad, grad_gate, grad_up, grad_down)


def solution(mesh):
    placed = (
        P(("expert", "dp"), None),
        P(("expert", "dp"), None),
        P(("expert", "dp"), None),
        P(("expert", "dp"), None),
        P("expert", None, ("dp", "shadow")),
        P("expert", None, ("dp", "shadow")),
        P("expert", ("dp", "shadow"), None),
    )
    return jax.shard_map(
        on_device,
        mesh=mesh,
        in_specs=placed,
        out_specs=(
            P(("expert", "dp"), None),
            P("expert", None, ("dp", "shadow")),
            P("expert", None, ("dp", "shadow")),
            P("expert", ("dp", "shadow"), None),
        ),
        check_vma=False,
    )
```
